32 devices in a mesh: row: 8 (over z, x), col: 4 (over y, core).
Axes of the slice: x: 2, y: 2, z: 4, core: 2. Of those that a mesh axis runs over, the one named last changes fastest.
Arguments:
- inputs: bfloat16 [768, 8192], P('col', 'row'), may hold values from -6 to 6
- cotangent: bfloat16 [768, 8192], P('col', 'row'), may hold values from -6 to 6
- query_weight: bfloat16 [2, 768, 768], P(None, 'row', 'col'), may hold values from -0.21875 to 0.21875
- key_weight: bfloat16 [2, 768, 768], P(None, 'row', 'col'), may hold values from -0.21875 to 0.21875
- value_weight: bfloat16 [2, 768, 768], P(None, 'row', 'col'), may hold values from -0.21875 to 0.21875
- out_weight: bfloat16 [2, 768, 768], P(None, 'row', 'col'), may hold values from -1.75 to 1.75
- query_bias: bfloat16 [2, 4, 192], P(None, 'col', 'row'), may hold values from -4 to 4
- value_bias: bfloat16 [2, 4, 192], P(None, 'col', 'row'), may hold values from -1.5 to 1.5
- out_bias: bfloat16 [2, 4, 192], P(None, 'col', 'row'), may hold values from -4 to 4
- attention_gain: bfloat16 [2, 768], replicated, may hold values from 0.5 to 1.5
- attention_shift: bfloat16 [2, 768], replicated, may hold values from -4 to 4
- expand_weight: bfloat16 [2, 768, 3072], P(None, 'row', 'col'), may hold values from -0.21875 to 0.21875
- expand_bias: bfloat16 [2, 4, 768], P(None, 'col', 'row'), may hold values from -6 to 6
- contract_weight: bfloat16 [2, 768, 3072], P(None, 'row', 'col'), may hold values from -0.109375 to 0.109375
- contract_bias: bfloat16 [2, 4, 192], P(None, 'col', 'row'), may hold values from -4 to 4
- feed_gain: bfloat16 [2, 768], replicated, may hold values from 0.5 to 1.5
- feed_shift: bfloat16 [2, 768], replicated, may hold values from -4 to 4
Outputs:
- outputs: bfloat16 [768, 8192], P('col', 'row')
- inputs_grad: float32 [768, 8192], P('col', 'row')
- query_weight_grad: float32 [2, 768, 768], P(None, 'row', 'col')
- key_weight_grad: float32 [2, 768, 768], P(None, 'row', 'col')
- value_weight_grad: float32 [2, 768, 768], P(None, 'row', 'col')
- out_weight_grad: float32 [2, 768, 768], P(None, 'row', 'col')
- query_bias_grad: float32 [2, 4, 192], P(None, 'col', 'row')
- value_bias_grad: float32 [2, 4, 192], P(None, 'col', 'row')
- out_bias_grad: float32 [2, 4, 192], P(None, 'col', 'row')
- attention_gain_grad: float32 [2, 4, 192], P(None, 'col', 'row')
- attention_shift_grad: float32 [2, 4, 192], P(None, 'col', 'row')
- expand_weight_grad: float32 [2, 768, 3072], P(None, 'row', 'col')
- expand_bias_grad: float32 [2, 4, 768], P(None, 'col', 'row')
- contract_weight_grad: float32 [2, 768, 3072], P(None, 'row', 'col')
- contract_bias_grad: float32 [2, 4, 192], P(None, 'col', 'row')
- feed_gain_grad: float32 [2, 4, 192], P(None, 'col', 'row')
- feed_shift_grad: float32 [2, 4, 192], P(None, 'col', 'row')
The draws below stay inside these ranges and needn't reach their ends.
All inputs are finite; a program needn't handle non-finite values.
Results may differ from the reference program's by a relative error of at most 0.023.
Values may be sent and summed in bfloat16 or wider, within the bound.
A program may use at most 192 MiB of HBM per device.

```python
import jax
import jax.numpy as jnp
from jax import lax

D = 768
H = 12
HD = 64
FF = 3072
SEQ = 1024
LAYERS = 2
NSEQ = 8
TOKENS = 8192
DCOL = 192
FCOL = 768
N_COL = 4


def block_scale(stream_key, extent, cuts, smallest, high):
    loudness, own = 1.0, jax.random.fold_in(stream_key, 6)
    for axis_at, parts in cuts:
        draws = jnp.exp(jax.random.uniform(jax.random.fold_in(own, axis_at), (parts,), jnp.float32, smallest / len(cuts), high / len(cuts)))
        loudness = loudness * jnp.repeat(draws, extent[axis_at] // parts).reshape([-1 if axis == axis_at else 1 for axis in range(len(extent))])
    return loudness


def bell_draw(key, shape, spread, reach, cuts=(), kind=jnp.bfloat16):
    level = block_scale(key, shape, cuts, -0.22, 0.18) if cuts else 1.0
    entries = jax.random.normal(key, shape, jnp.float32) * spread * level
    return jnp.minimum(jnp.maximum(entries, -reach), reach).astype(kind)


def setup_inputs(seed: int = 0) -> dict:
    key_of = jax.random.split(jax.random.key(seed), 18)
    inputs = bell_draw(key_of[0], (D, TOKENS), 1.0, 6.0, ((0, 4), (1, 8)))
    cotangent = bell_draw(key_of[1], (D, TOKENS), 1.0, 6.0, ((0, 4), (1, 8)))
    query_weight = bell_draw(key_of[2], (LAYERS, D, D), D ** -0.5, 0.21875, ((1, 8), (2, 4)))
    key_weight = bell_draw(key_of[3], (LAYERS, D, D), D ** -0.5, 0.21875, ((1, 8), (2, 4)))
    value_weight = bell_draw(key_of[4], (LAYERS, D, D), D ** -0.5, 0.21875, ((1, 8), (2, 4)))
    out_weight = bell_draw(key_of[5], (LAYERS, D, D), (D // 64) ** -0.5, 1.75, ((1, 8), (2, 4)))
    query_bias = bell_draw(key_of[6], (LAYERS, N_COL, DCOL), 0.3, 4.0, ((1, 4), (2, 8)))
    value_bias = bell_draw(key_of[7], (LAYERS, N_COL, DCOL), 0.1, 1.5, ((1, 4), (2, 8)))
    out_bias = bell_draw(key_of[8], (LAYERS, N_COL, DCOL), 0.3, 4.0, ((1, 4), (2, 8)))
    attention_gain = jnp.clip(1.0 + 0.1 * jax.random.normal(key_of[9], (LAYERS, D), jnp.float32), 0.5, 1.5).astype(jnp.bfloat16)
    attention_shift = bell_draw(key_of[10], (LAYERS, D), 0.3, 4.0)
    expand_weight = bell_draw(key_of[11], (LAYERS, D, FF), D ** -0.5, 0.21875, ((1, 8), (2, 4)))
    expand_bias = bell_draw(key_of[12], (LAYERS, N_COL, FCOL), 0.5, 6.0, ((1, 4), (2, 8)))
    contract_weight = bell_draw(key_of[13], (LAYERS, D, FF), FF ** -0.5, 0.109375, ((1, 8), (2, 4)))
    contract_bias = bell_draw(key_of[14], (LAYERS, N_COL, DCOL), 0.3, 4.0, ((1, 4), (2, 8)))
    feed_gain = jnp.clip(1.0 + 0.1 * jax.random.normal(key_of[15], (LAYERS, D), jnp.float32), 0.5, 1.5).astype(jnp.bfloat16)
    feed_shift = bell_draw(key_of[16], (LAYERS, D), 0.3, 4.0)
    return dict(inputs=inputs, cotangent=cotangent, query_weight=query_weight, key_weight=key_weight, value_weight=value_weight, out_weight=out_weight, query_bias=query_bias, value_bias=value_bias, out_bias=out_bias, attention_gain=attention_gain, attention_shift=attention_shift, expand_weight=expand_weight, expand_bias=expand_bias, contract_weight=contract_weight, contract_bias=contract_bias, feed_gain=feed_gain, feed_shift=feed_shift)


EPSILON = 1e-05
HIGHEST = lax.Precision.HIGHEST

@jax.custom_vjp
def low(v):
    return lax.optimization_barrier(v.astype(jnp.bfloat16)).astype(jnp.float32)

@jax.custom_vjp
def low_back(v):
    return v

def low_keep(v):
    return (low(v), None)

def low_pass(kept, grad):
    return (grad,)

def back_keep(v):
    return (v, None)

def back_low(kept, grad):
    return (low(grad),)
low.defvjp(low_keep, low_pass)
low_back.defvjp(back_keep, back_low)

def matmul(left, right):
    return jnp.dot(left, right, precision=HIGHEST)

def layer_norm(rows_in, gain_row, shift_row):
    row_mean = lax.optimization_barrier(jnp.mean(rows_in, axis=-1, keepdims=True))
    centred = rows_in - row_mean
    row_var = lax.optimization_barrier(jnp.mean(centred * centred, axis=-1, keepdims=True))
    return centred * lax.rsqrt(row_var + EPSILON) * gain_row + shift_row

def gelu_tanh(values):
    return 0.5 * values * (1.0 + jnp.tanh(0.7978845608028654 * (values + 0.044715 * values * values * values)))

def attend_sequence(block_in):
    query_seq, key_seq, value_seq = block_in
    scores = low_back(jnp.einsum('qhd,khd->hqk', query_seq, key_seq, precision=HIGHEST) * 0.125)
    positions = jnp.arange(SEQ)
    allowed = positions[:, None] >= positions[None, :]
    scores = jnp.where(allowed[None], scores, -1e+30)
    row_top = lax.optimization_barrier(jnp.max(scores, axis=-1, keepdims=True))
    weights = jnp.exp(scores - row_top)
    prob_rows = weights / lax.optimization_barrier(jnp.sum(weights, axis=-1, keepdims=True))
    return jnp.einsum('hqk,khd->qhd', low(prob_rows), value_seq, precision=HIGHEST)

def forward(resid, query_weight, key_weight, value_weight, out_weight, query_bias, value_bias, out_bias, attention_gain, attention_shift, expand_weight, expand_bias, contract_weight, contract_bias, feed_gain, feed_shift):
    head_shape = (NSEQ, SEQ, H, HD)
    for layer_idx in range(LAYERS):
        norm_one = low(layer_norm(resid, attention_gain[layer_idx], attention_shift[layer_idx]))
        query_rows = low(low_back(matmul(norm_one, query_weight[layer_idx]) + query_bias[layer_idx]))
        key_rows = low(low_back(matmul(norm_one, key_weight[layer_idx])))
        value_rows = low(low_back(matmul(norm_one, value_weight[layer_idx]) + value_bias[layer_idx]))
        mixed_rows = lax.map(jax.checkpoint(attend_sequence), (query_rows.reshape(head_shape), key_rows.reshape(head_shape), value_rows.reshape(head_shape)))
        mixed_rows = low(low_back(mixed_rows.reshape(TOKENS, D)))
        resid = resid + low_back(matmul(mixed_rows, out_weight[layer_idx].T) + out_bias[layer_idx])
        norm_two = low(layer_norm(resid, feed_gain[layer_idx], feed_shift[layer_idx]))
        before_act = low_back(matmul(norm_two, expand_weight[layer_idx]) + expand_bias[layer_idx])
        hidden_rows = low(gelu_tanh(before_act))
        resid = resid + low_back(matmul(hidden_rows, contract_weight[layer_idx].T) + contract_bias[layer_idx])
    return resid

def reference(inputs, cotangent, query_weight, key_weight, value_weight, out_weight, query_bias, value_bias, out_bias, attention_gain, attention_shift, expand_weight, expand_bias, contract_weight, contract_bias, feed_gain, feed_shift):

    def widen(array_in, full_width):
        return array_in.astype(jnp.float32).reshape(LAYERS, full_width)

    def narrow(array_in):
        return array_in.reshape(LAYERS, N_COL, array_in.shape[1] // N_COL)
    result_rows, pull_back = jax.vjp(forward, inputs.astype(jnp.float32).T, query_weight.astype(jnp.float32), key_weight.astype(jnp.float32), value_weight.astype(jnp.float32), out_weight.astype(jnp.float32), widen(query_bias, D), widen(value_bias, D), widen(out_bias, D), attention_gain.astype(jnp.float32), attention_shift.astype(jnp.float32), expand_weight.astype(jnp.float32), widen(expand_bias, FF), contract_weight.astype(jnp.float32), widen(contract_bias, D), feed_gain.astype(jnp.float32), feed_shift.astype(jnp.float32))
    grads = pull_back(cotangent.astype(jnp.float32).T)
    return (result_rows.astype(jnp.bfloat16).T, grads[0].T, grads[1], grads[2], grads[3], grads[4], narrow(grads[5]), narrow(grads[6]), narrow(grads[7]), narrow(grads[8]), narrow(grads[9]), grads[10], narrow(grads[11]), grads[12], narrow(grads[13]), narrow(grads[14]), narrow(grads[15]))
```

```python
import jax
import jax.numpy as jnp
from jax import lax
from jax.sharding import PartitionSpec as P

HD = 64
SEQ = 1024


EPSILON = 1e-05
NEG_FILL = -1e30


def contract_rows(left, right):
    return lax.dot_general(
        left, right, (((0,), (0,)), ((), ())), preferred_element_type=jnp.float32
    )


def contract_cols(left, right):
    return lax.dot_general(
        left, right, (((1,), (1,)), ((), ())), preferred_element_type=jnp.float32
    )


def gelu_tanh(values):
    return (
        0.5
        * values
        * (1.0 + jnp.tanh(0.7978845608028654 * (values + 0.044715 * values * values * values)))
    )


def col_gather(rows_in):
    return lax.all_gather(rows_in, "col", axis=0, tiled=True)


def col_scatter(partial_rows):
    return lax.psum_scatter(
        partial_rows.astype(jnp.bfloat16), "col", scatter_dimension=0, tiled=True
    ).astype(jnp.float32)


def own_rows(rows_in):
    count = rows_in.shape[0] // lax.axis_size("col")
    return lax.dynamic_slice_in_dim(rows_in, lax.axis_index("col") * count, count, 0)


def own_features(rows_in):
    width = rows_in.shape[-1] // lax.axis_size("col")
    return lax.dynamic_slice_in_dim(
        rows_in, lax.axis_index("col") * width, width, rows_in.ndim - 1
    )


def spread_bias(bias_share, full_width):
    return lax.dynamic_update_slice_in_dim(
        jnp.zeros((full_width,), jnp.float32),
        bias_share.astype(jnp.float32),
        lax.axis_index("col") * bias_share.shape[0],
        0,
    )


def norm_unit(rows_in):
    row_mean = jnp.mean(rows_in, axis=1, keepdims=True)
    centred = rows_in - row_mean
    inv_std = lax.rsqrt(jnp.mean(centred * centred, axis=1, keepdims=True) + EPSILON)
    return centred * inv_std, inv_std


def norm_apply(unit_rows, gain, shift):
    return (unit_rows * gain + shift).astype(jnp.bfloat16)


def norm_back(normed_grad, unit_rows, inv_std, gain):
    scaled = normed_grad * gain
    first = jnp.mean(scaled, axis=1, keepdims=True)
    second = jnp.mean(scaled * unit_rows, axis=1, keepdims=True)
    back_rows = inv_std * (scaled - first - unit_rows * second)
    return back_rows, jnp.sum(normed_grad * unit_rows, axis=0), jnp.sum(normed_grad, axis=0)


def token_sum(rows_in):
    return jnp.sum(rows_in.astype(jnp.float32), axis=0)


def by_row(vector):
    return vector.reshape(lax.axis_size("row"), -1)


def row_total(packed):
    return lax.psum_scatter(
        packed.astype(jnp.bfloat16), "row", scatter_dimension=0, tiled=True
    ).astype(jnp.float32)


def local(
    inputs,
    cotangent,
    query_weight,
    key_weight,
    value_weight,
    out_weight,
    query_bias,
    value_bias,
    out_bias,
    attention_gain,
    attention_shift,
    expand_weight,
    expand_bias,
    contract_weight,
    contract_bias,
    feed_gain,
    feed_shift,
):
    layer_count, slab, part = query_weight.shape
    hidden_part = expand_weight.shape[2]
    row_count = lax.axis_size("row")
    width = slab * row_count
    bias_pack = jnp.concatenate(
        [
            item.reshape(layer_count, -1)
            for item in (query_bias, value_bias, out_bias, contract_bias, expand_bias)
        ],
        axis=1,
    )
    bias_len = bias_pack.size
    attn_width = 4 * part
    bias_rows = -(-bias_len // (attn_width * 16)) * 16
    bias_block = jnp.pad(
        bias_pack.reshape(-1), (0, bias_rows * attn_width - bias_len)
    ).reshape(bias_rows, attn_width)

    def attn_slab(layer_idx):
        return jnp.concatenate(
            [
                query_weight[layer_idx],
                key_weight[layer_idx],
                value_weight[layer_idx],
                out_weight[layer_idx],
            ],
            axis=1,
        )

    first_pack = lax.all_gather(
        jnp.concatenate([attn_slab(0), bias_block], axis=0), "row", axis=0
    )
    gathered_bias = (
        first_pack[:, slab:].reshape(row_count, -1)[:, :bias_len].reshape(row_count, layer_count, -1)
    )
    small = part // row_count
    rest = [("feed", 0)]
    for layer_idx in range(1, layer_count):
        rest += [("attn", layer_idx), ("feed", layer_idx)]
    feed_slabs = [
        jnp.concatenate([expand_weight[item], contract_weight[item]], axis=1)
        for item in range(layer_count)
    ]
    attn_w = [first_pack[:, :slab].reshape(width, attn_width)]
    feed_w = [lax.all_gather(feed_slabs[0], "row", axis=0, tiled=True)]
    for layer_idx in range(1, layer_count):
        both = lax.all_gather(
            jnp.concatenate([attn_slab(layer_idx), feed_slabs[layer_idx]], axis=1),
            "row",
            axis=0,
            tiled=True,
        )
        attn_w.append(both[:, :attn_width])
        feed_w.append(both[:, attn_width:])

    def bias_of(layer_idx, start, count):
        return gathered_bias[:, layer_idx, start : start + count].reshape(-1)

    x_full = lax.all_gather(inputs, "col", axis=0, tiled=True).T
    cot_full = lax.all_gather(cotangent, "col", axis=0, tiled=True).T
    resid = own_rows(x_full).astype(jnp.float32)
    saved = []
    for layer_idx in range(layer_count):
        w_attn, w_feed = attn_w[layer_idx], feed_w[layer_idx]
        w_qkv, w_out = w_attn[:, : 3 * part], w_attn[:, 3 * part :]
        w_expand, w_contract = w_feed[:, :hidden_part], w_feed[:, hidden_part:]
        b_query = bias_of(layer_idx, 0, small).astype(jnp.float32)
        b_value = bias_of(layer_idx, small, small).astype(jnp.float32)
        b_out = bias_of(layer_idx, 2 * small, small)
        b_contract = bias_of(layer_idx, 3 * small, small)
        b_expand = bias_of(layer_idx, 4 * small, hidden_part // row_count)
        gain_one = attention_gain[layer_idx].astype(jnp.float32)
        shift_one = attention_shift[layer_idx].astype(jnp.float32)
        gain_two = feed_gain[layer_idx].astype(jnp.float32)
        shift_two = feed_shift[layer_idx].astype(jnp.float32)
        unit_one, inv_one = norm_unit(resid)
        if layer_idx == 0:
            norm_one = norm_apply(norm_unit(x_full.astype(jnp.float32))[0], gain_one, shift_one)
        else:
            norm_one = col_gather(norm_apply(unit_one, gain_one, shift_one))
        b_qkv = jnp.concatenate([b_query, jnp.zeros_like(b_query), b_value])
        qkv = (jnp.dot(norm_one, w_qkv, preferred_element_type=jnp.float32) + b_qkv).astype(
            jnp.bfloat16
        )
        query_rows, key_rows, value_rows = (
            qkv[:, :part],
            qkv[:, part : 2 * part],
            qkv[:, 2 * part :],
        )
        mixed_rows, log_totals = attend(query_rows, key_rows, value_rows)
        resid = resid + col_scatter(contract_cols(mixed_rows, w_out) + spread_bias(b_out, width))
        unit_two, inv_two = norm_unit(resid)
        norm_two = col_gather(norm_apply(unit_two, gain_two, shift_two))
        before_act = jnp.dot(norm_two, w_expand, preferred_element_type=jnp.float32) + b_expand
        hidden_rows = gelu_tanh(before_act).astype(jnp.bfloat16)
        partial_rows = contract_cols(hidden_rows, w_contract) + spread_bias(b_contract, width)
        if layer_idx + 1 < layer_count:
            resid = resid + col_scatter(partial_rows)
        else:
            count = resid.shape[0]
            start = lax.axis_index("col") * count
            mine = lax.dynamic_slice_in_dim(partial_rows, start, count, 0) + resid
            partial_rows = lax.dynamic_update_slice_in_dim(partial_rows, mine, start, 0)
            outputs = lax.psum_scatter(
                partial_rows.astype(jnp.bfloat16), "col", scatter_dimension=1, tiled=True
            ).T
        saved.append(
            (
                (w_qkv, w_out, w_expand, w_contract, gain_one, gain_two),
                (norm_one, unit_one, inv_one, query_rows, key_rows, value_rows),
                (mixed_rows, log_totals, norm_two, unit_two, inv_two, before_act, hidden_rows),
            )
        )
    grad = own_rows(cot_full).astype(jnp.float32)
    branch_full = cot_full
    packs = [None] * layer_count
    vectors = [None] * layer_count
    norm_sums = [None] * layer_count
    for layer_idx in reversed(range(layer_count)):
        (
            (w_qkv, w_out, w_expand, w_contract, gain_one, gain_two),
            (norm_one, unit_one, inv_one, query_rows, key_rows, value_rows),
            (mixed_rows, log_totals, norm_two, unit_two, inv_two, before_act, hidden_rows),
        ) = saved[layer_idx]
        d_hidden = jnp.dot(branch_full, w_contract, preferred_element_type=jnp.float32)
        d_before = jax.vjp(gelu_tanh, before_act)[1](d_hidden)[0].astype(jnp.bfloat16)
        d_norm = col_scatter(contract_cols(d_before, w_expand))
        contract_part = contract_rows(branch_full, hidden_rows)
        expand_part = contract_rows(norm_two, d_before)
        contract_bias_part = token_sum(own_features(branch_full))
        back_rows, gain_two_part, shift_two_part = norm_back(d_norm, unit_two, inv_two, gain_two)
        grad = grad + back_rows
        branch_full = col_gather(grad.astype(jnp.bfloat16))
        d_mixed = jnp.dot(branch_full, w_out, preferred_element_type=jnp.float32).astype(
            jnp.bfloat16
        )
        out_part = contract_rows(branch_full, mixed_rows)
        out_bias_part = token_sum(own_features(branch_full))
        d_query, d_key, d_value = attend_back(query_rows, key_rows, value_rows, log_totals, d_mixed)
        d_qkv = jnp.concatenate([d_query, d_key, d_value], axis=1)
        d_norm = col_scatter(contract_cols(d_qkv, w_qkv))
        qkv_part = contract_rows(norm_one, d_qkv)
        back_rows, gain_one_part, shift_one_part = norm_back(d_norm, unit_one, inv_one, gain_one)
        grad = grad + back_rows
        branch_full = col_gather(grad.astype(jnp.bfloat16))
        packs[layer_idx] = jnp.concatenate([qkv_part, out_part, expand_part, contract_part], axis=1)
        vectors[layer_idx] = (
            token_sum(d_query),
            token_sum(d_value),
            out_bias_part,
            token_sum(d_before),
            contract_bias_part,
        )
        norm_sums[layer_idx] = jnp.stack(
            [gain_one_part, shift_one_part, gain_two_part, shift_two_part]
        )
    inputs_grad = own_features(branch_full).astype(jnp.float32).T
    norm_total = own_features(lax.psum(jnp.stack(norm_sums), "col"))
    flat = []
    for layer_idx in range(layer_count):
        flat += [by_row(item) for item in vectors[layer_idx]]
        flat += [by_row(norm_total[layer_idx, item]) for item in range(4)]
    sizes = [item.shape[1] for item in flat]
    flat = jnp.concatenate(flat, axis=1)
    pack_width = packs[0].shape[1]
    extra = -(-flat.shape[1] // (pack_width * 16)) * 16
    flat = jnp.pad(flat, ((0, 0), (0, extra * pack_width - flat.shape[1])))
    last_pack = jnp.concatenate(
        [
            packs[0].reshape(row_count, slab, pack_width),
            flat.reshape(row_count, extra, pack_width),
        ],
        axis=1,
    )
    last_total = row_total(last_pack)[0]
    totals = [last_total[:slab]] + [row_total(packs[item]) for item in range(1, layer_count)]
    loose = last_total[slab:].reshape(-1)
    pieces = []
    start = 0
    for size in sizes:
        pieces.append(loose[start : start + size])
        start += size

    def weight_grad(start, count):
        return jnp.stack([item[:, start : start + count] for item in totals])

    def vector_grad(member):
        return jnp.stack([pieces[layer * 9 + member].reshape(1, -1) for layer in range(layer_count)])

    return (
        outputs,
        inputs_grad,
        weight_grad(0, part),
        weight_grad(part, part),
        weight_grad(2 * part, part),
        weight_grad(3 * part, part),
        vector_grad(0),
        vector_grad(1),
        vector_grad(2),
        vector_grad(5),
        vector_grad(6),
        weight_grad(4 * part, hidden_part),
        vector_grad(3),
        weight_grad(4 * part + hidden_part, hidden_part),
        vector_grad(4),
        vector_grad(7),
        vector_grad(8),
    )


def split_heads(rows_in):
    return rows_in.reshape(rows_in.shape[0] // SEQ, SEQ, rows_in.shape[1] // HD, HD)


def causal_scores(query_block, key_block, row_begin):
    scores = (
        jnp.einsum("sqhd,skhd->shqk", query_block, key_block, preferred_element_type=jnp.float32)
        * 0.125
    )
    grid_shape = (query_block.shape[1], key_block.shape[1])
    row_ids = row_begin + lax.broadcasted_iota(jnp.int32, grid_shape, 0)
    col_ids = lax.broadcasted_iota(jnp.int32, grid_shape, 1)
    return jnp.where((row_ids >= col_ids)[None, None], scores, NEG_FILL)


def attend(query_rows, key_rows, value_rows):
    block_rows = min(512, SEQ)
    query_seq = split_heads(query_rows)
    key_seq = split_heads(key_rows)
    value_seq = split_heads(value_rows)
    out_blocks = []
    log_totals = []
    for row_begin in range(0, SEQ, block_rows):
        row_end = row_begin + block_rows
        scores = causal_scores(query_seq[:, row_begin:row_end], key_seq[:, :row_end], row_begin)
        row_top = jnp.max(scores, axis=-1, keepdims=True)
        weights = jnp.exp(scores - row_top)
        row_total = jnp.sum(weights, axis=-1, keepdims=True)
        prob_rows = (weights / row_total).astype(jnp.bfloat16)
        out_blocks.append(
            jnp.einsum(
                "shqk,skhd->sqhd",
                prob_rows,
                value_seq[:, :row_end],
                preferred_element_type=jnp.float32,
            )
        )
        log_totals.append(row_top + jnp.log(row_total))
    mixed_rows = jnp.concatenate(out_blocks, axis=1).reshape(query_rows.shape).astype(jnp.bfloat16)
    return (mixed_rows, log_totals)


def attend_back(query_rows, key_rows, value_rows, log_totals, d_mixed):
    block_rows = min(512, SEQ)
    query_seq = split_heads(query_rows)
    key_seq = split_heads(key_rows)
    value_seq = split_heads(value_rows)
    grad_seq = split_heads(d_mixed)
    d_query_blocks = []
    d_key_seq = jnp.zeros(key_seq.shape, jnp.float32)
    d_value_seq = jnp.zeros(value_seq.shape, jnp.float32)
    for block_idx, row_begin in enumerate(range(0, SEQ, block_rows)):
        row_end = row_begin + block_rows
        tail_pad = ((0, 0), (0, SEQ - row_end), (0, 0), (0, 0))
        scores = causal_scores(query_seq[:, row_begin:row_end], key_seq[:, :row_end], row_begin)
        prob_rows = jnp.exp(scores - log_totals[block_idx])
        grad_block = grad_seq[:, row_begin:row_end]
        d_probs = jnp.einsum(
            "sqhd,skhd->shqk",
            grad_block,
            value_seq[:, :row_end],
            preferred_element_type=jnp.float32,
        )
        d_value_seq = d_value_seq + jnp.pad(
            jnp.einsum(
                "shqk,sqhd->skhd",
                prob_rows.astype(jnp.bfloat16),
                grad_block,
                preferred_element_type=jnp.float32,
            ),
            tail_pad,
        )
        inner_sum = jnp.sum(d_probs * prob_rows, axis=-1, keepdims=True)
        d_scores = (prob_rows * (d_probs - inner_sum)).astype(jnp.bfloat16)
        d_query_blocks.append(
            jnp.einsum(
                "shqk,skhd->sqhd",
                d_scores,
                key_seq[:, :row_end],
                preferred_element_type=jnp.float32,
            )
            * 0.125
        )
        d_key_seq = d_key_seq + jnp.pad(
            jnp.einsum(
                "shqk,sqhd->skhd",
                d_scores,
                query_seq[:, row_begin:row_end],
                preferred_element_type=jnp.float32,
            )
            * 0.125,
            tail_pad,
        )
    rows_shape = query_rows.shape
    d_query = jnp.concatenate(d_query_blocks, axis=1).reshape(rows_shape).astype(jnp.bfloat16)
    return (
        d_query,
        d_key_seq.reshape(rows_shape).astype(jnp.bfloat16),
        d_value_seq.reshape(rows_shape).astype(jnp.bfloat16),
    )


def solution(mesh):
    placed = (
        P("col", "row"),
        P("col", "row"),
        P(None, "row", "col"),
        P(None, "row", "col"),
        P(None, "row", "col"),
        P(None, "row", "col"),
        P(None, "col", "row"),
        P(None, "col", "row"),
        P(None, "col", "row"),
        P(),
        P(),
        P(None, "row", "col"),
        P(None, "col", "row"),
        P(None, "row", "col"),
        P(None, "col", "row"),
        P(),
        P(),
    )
    return jax.shard_map(
        local,
        mesh=mesh,
        in_specs=placed,
        out_specs=(
            P("col", "row"),
            P("col", "row"),
            P(None, "row", "col"),
            P(None, "row", "col"),
            P(None, "row", "col"),
            P(None, "row", "col"),
            P(None, "col", "row"),
            P(None, "col", "row"),
            P(None, "col", "row"),
            P(None, "col", "row"),
            P(None, "col", "row"),
            P(None, "row", "col"),
            P(None, "col", "row"),
            P(None, "row", "col"),
            P(None, "col", "row"),
            P(None, "col", "row"),
            P(None, "col", "row"),
        ),
        check_vma=False,
    )
```

```python
import functools

import jax
import jax.numpy as jnp
from jax import lax
from jax.experimental import pallas as pl
from jax.experimental.pallas import tpu as pltpu
from jax.sharding import PartitionSpec as P

HD = 64
SEQ = 1024


EPSILON = 1e-05
NEG_FILL = -1e30


def contract_rows(left, right):
    return lax.dot_general(
        left, right, (((0,), (0,)), ((), ())), preferred_element_type=jnp.float32
    )


def contract_cols(left, right):
    return lax.dot_general(
        left, right, (((1,), (1,)), ((), ())), preferred_element_type=jnp.float32
    )


def gelu_tanh(values):
    return (
        0.5
        * values
        * (1.0 + jnp.tanh(0.7978845608028654 * (values + 0.044715 * values * values * values)))
    )


def col_gather(rows_in):
    return lax.all_gather(rows_in, "col", axis=0, tiled=True)


def col_scatter(partial_rows):
    return lax.psum_scatter(
        partial_rows.astype(jnp.bfloat16), "col", scatter_dimension=0, tiled=True
    ).astype(jnp.float32)


def own_rows(rows_in):
    count = rows_in.shape[0] // lax.axis_size("col")
    return lax.dynamic_slice_in_dim(rows_in, lax.axis_index("col") * count, count, 0)


def own_features(rows_in):
    width = rows_in.shape[-1] // lax.axis_size("col")
    return lax.dynamic_slice_in_dim(
        rows_in, lax.axis_index("col") * width, width, rows_in.ndim - 1
    )


def spread_bias(bias_share, full_width):
    return lax.dynamic_update_slice_in_dim(
        jnp.zeros((full_width,), jnp.float32),
        bias_share.astype(jnp.float32),
        lax.axis_index("col") * bias_share.shape[0],
        0,
    )


def norm_unit(rows_in):
    row_mean = jnp.mean(rows_in, axis=1, keepdims=True)
    centred = rows_in - row_mean
    inv_std = lax.rsqrt(jnp.mean(centred * centred, axis=1, keepdims=True) + EPSILON)
    return centred * inv_std, inv_std


def norm_apply(unit_rows, gain, shift):
    return (unit_rows * gain + shift).astype(jnp.bfloat16)


def norm_back(normed_grad, unit_rows, inv_std, gain):
    scaled = normed_grad * gain
    first = jnp.mean(scaled, axis=1, keepdims=True)
    second = jnp.mean(scaled * unit_rows, axis=1, keepdims=True)
    back_rows = inv_std * (scaled - first - unit_rows * second)
    return back_rows, jnp.sum(normed_grad * unit_rows, axis=0), jnp.sum(normed_grad, axis=0)


def token_sum(rows_in):
    return jnp.sum(rows_in.astype(jnp.float32), axis=0)


def exchange_body(kind, chunks, *refs):
    if kind == "forward":
        partial, carry, gain, shift, carry_out, full, unit_out, inv_out = refs[:8]
        scratch = refs[8:]
    else:
        partial, carry, gain, unit, inv, carry_out, full, gain_out, shift_out = refs[:9]
        scratch = refs[9:]
    from_pair, pair_sum, from_far = scratch[:3]
    (near_s, near_r, far_s, far_r, gy_s, gy_r, gc_s, gc_r, fw_s, fw_r) = scratch[3:]
    rows = carry.shape[0]
    step = rows // chunks
    me = lax.axis_index("col")
    pair = me + 1 - 2 * (me % 2)
    far = (me + 2) % 4
    corner = (pair + 2) % 4

    def at(block, chunk):
        return pl.ds(pl.multiple_of(block * rows + chunk * step, step), step)

    def send(src, dst, send_sem, recv_sem, target):
        return pltpu.make_async_remote_copy(
            src_ref=src,
            dst_ref=dst,
            send_sem=send_sem,
            recv_sem=recv_sem,
            device_id={"col": target},
            device_id_type=pl.DeviceIdType.MESH,
        )

    barrier = pltpu.get_barrier_semaphore()
    for other in (pair, far):
        pl.semaphore_signal(
            barrier, inc=1, device_id={"col": other}, device_id_type=pl.DeviceIdType.MESH
        )
    pl.semaphore_wait(barrier, 2)
    near = []
    for half, owner in enumerate((corner, pair)):
        for chunk in range(chunks):
            slot = half * chunks + chunk
            copy = send(
                partial.at[at(owner, chunk)],
                from_pair.at[pl.ds(slot * step, step)],
                near_s.at[slot],
                near_r.at[slot],
                pair,
            )
            copy.start()
            near.append(copy)
    over = []
    for chunk in range(chunks):
        near[chunk].wait_recv()
        here = pl.ds(chunk * step, step)
        pair_sum[here] = (
            partial[at(far, chunk)].astype(jnp.float32) + from_pair[here].astype(jnp.float32)
        ).astype(jnp.bfloat16)
        copy = send(pair_sum.at[here], from_far.at[here], far_s.at[chunk], far_r.at[chunk], far)
        copy.start()
        over.append(copy)
    if kind == "backward":
        gain_sum = jnp.zeros((1, carry.shape[1]), jnp.float32)
        shift_sum = jnp.zeros((1, carry.shape[1]), jnp.float32)
    across = []
    beside = []
    for chunk in range(chunks):
        near[chunks + chunk].wait_recv()
        over[chunk].wait_recv()
        here = pl.ds(chunk * step, step)
        total = (
            partial[at(me, chunk)].astype(jnp.float32)
            + from_pair[pl.ds((chunks + chunk) * step, step)].astype(jnp.float32)
            + from_far[here].astype(jnp.float32)
        )
        if kind == "forward":
            value = carry[here] + total
            carry_out[here] = value
            unit_rows, inv_std = norm_unit(value)
            unit_out[here] = unit_rows
            inv_out[here] = jnp.broadcast_to(inv_std, (step, inv_out.shape[1]))
            result = norm_apply(unit_rows, gain[...], shift[...])
        else:
            unit_rows = unit[here]
            gain_sum = gain_sum + jnp.sum(total * unit_rows, axis=0, keepdims=True)
            shift_sum = shift_sum + jnp.sum(total, axis=0, keepdims=True)
            scaled = total * gain[...]
            first = jnp.mean(scaled, axis=1, keepdims=True)
            second = jnp.mean(scaled * unit_rows, axis=1, keepdims=True)
            value = carry[here] + inv[here][:, :1] * (scaled - first - unit_rows * second)
            carry_out[here] = value
            result = value.astype(jnp.bfloat16)
        mine = at(me, chunk)
        full[mine] = result
        copy = send(full.at[mine], full.at[mine], gy_s.at[chunk], gy_r.at[chunk], far)
        copy.start()
        across.append(copy)
        copy = send(full.at[mine], full.at[mine], gc_s.at[chunk], gc_r.at[chunk], pair)
        copy.start()
        beside.append(copy)
    if kind == "backward":
        gain_out[...] = gain_sum
        shift_out[...] = shift_sum
    onward = []
    for chunk in range(chunks):
        across[chunk].wait_recv()
        spot = at(far, chunk)
        copy = send(full.at[spot], full.at[spot], fw_s.at[chunk], fw_r.at[chunk], pair)
        copy.start()
        onward.append(copy)
    for copy in beside + onward:
        copy.wait_recv()
    for copy in near + over + across + beside + onward:
        copy.wait_send()


def exchange(kind, partial, carry, *rest):
    rows, width = carry.shape
    chunks = 4
    wide = jax.ShapeDtypeStruct((rows, width), jnp.float32)
    outs = [wide, jax.ShapeDtypeStruct((4 * rows, width), jnp.bfloat16)]
    if kind == "forward":
        outs += [wide, jax.ShapeDtypeStruct((rows, 128), jnp.float32)]
    else:
        outs += [jax.ShapeDtypeStruct((1, width), jnp.float32)] * 2
    in_vmem = pl.BlockSpec(memory_space=pltpu.VMEM)
    dma = pltpu.SemaphoreType.DMA
    return pl.pallas_call(
        functools.partial(exchange_body, kind, chunks),
        out_shape=outs,
        in_specs=[in_vmem] * (2 + len(rest)),
        out_specs=[in_vmem] * len(outs),
        scratch_shapes=[
            pltpu.VMEM((2 * rows, width), jnp.bfloat16),
            pltpu.VMEM((rows, width), jnp.bfloat16),
            pltpu.VMEM((rows, width), jnp.bfloat16),
        ]
        + [dma((2 * chunks,))] * 2
        + [dma((chunks,))] * 8,
        cost_estimate=pl.CostEstimate(
            flops=20 * rows * width, bytes_accessed=50_000_000, transcendentals=0
        ),
        compiler_params=pltpu.CompilerParams(
            collective_id=1 if kind == "forward" else 2,
            has_side_effects=True,
            vmem_limit_bytes=32 * 1024 * 1024,
        ),
        name="exchange_" + kind,
    )(partial, carry, *rest)


def by_row(vector):
    return vector.reshape(lax.axis_size("row"), -1)


def row_total(packed):
    return lax.psum_scatter(
        packed.astype(jnp.bfloat16), "row", scatter_dimension=0, tiled=True
    ).astype(jnp.float32)


def local(
    inputs,
    cotangent,
    query_weight,
    key_weight,
    value_weight,
    out_weight,
    query_bias,
    value_bias,
    out_bias,
    attention_gain,
    attention_shift,
    expand_weight,
    expand_bias,
    contract_weight,
    contract_bias,
    feed_gain,
    feed_shift,
):
    layer_count, slab, part = query_weight.shape
    hidden_part = expand_weight.shape[2]
    row_count = lax.axis_size("row")
    width = slab * row_count
    bias_pack = jnp.concatenate(
        [
            item.reshape(layer_count, -1)
            for item in (query_bias, value_bias, out_bias, contract_bias, expand_bias)
        ],
        axis=1,
    )
    bias_len = bias_pack.size
    attn_width = 4 * part
    bias_rows = -(-bias_len // (attn_width * 16)) * 16
    bias_block = jnp.pad(
        bias_pack.reshape(-1), (0, bias_rows * attn_width - bias_len)
    ).reshape(bias_rows, attn_width)

    def attn_slab(layer_idx):
        return jnp.concatenate(
            [
                query_weight[layer_idx],
                key_weight[layer_idx],
                value_weight[layer_idx],
                out_weight[layer_idx],
            ],
            axis=1,
        )

    first_pack = lax.all_gather(
        jnp.concatenate([attn_slab(0), bias_block], axis=0), "row", axis=0
    )
    gathered_bias = (
        first_pack[:, slab:].reshape(row_count, -1)[:, :bias_len].reshape(row_count, layer_count, -1)
    )
    small = part // row_count
    rest = [("feed", 0)]
    for layer_idx in range(1, layer_count):
        rest += [("attn", layer_idx), ("feed", layer_idx)]
    feed_slabs = [
        jnp.concatenate([expand_weight[item], contract_weight[item]], axis=1)
        for item in range(layer_count)
    ]
    attn_w = [first_pack[:, :slab].reshape(width, attn_width)]
    feed_w = [lax.all_gather(feed_slabs[0], "row", axis=0, tiled=True)]
    for layer_idx in range(1, layer_count):
        both = lax.all_gather(
            jnp.concatenate([attn_slab(layer_idx), feed_slabs[layer_idx]], axis=1),
            "row",
            axis=0,
            tiled=True,
        )
        attn_w.append(both[:, :attn_width])
        feed_w.append(both[:, attn_width:])

    def bias_of(layer_idx, start, count):
        return gathered_bias[:, layer_idx, start : start + count].reshape(-1)

    x_full = lax.all_gather(inputs, "col", axis=0, tiled=True).T
    cot_full = lax.all_gather(cotangent, "col", axis=0, tiled=True).T
    resid = own_rows(x_full).astype(jnp.float32)
    unit_one, inv_one = norm_unit(resid)
    inv_one = jnp.broadcast_to(inv_one, (resid.shape[0], 128))
    gain_of = [item.astype(jnp.float32)[None] for item in attention_gain]
    shift_of = [item.astype(jnp.float32)[None] for item in attention_shift]
    norm_one = norm_apply(norm_unit(x_full.astype(jnp.float32))[0], gain_of[0], shift_of[0])
    saved = []
    for layer_idx in range(layer_count):
        w_attn, w_feed = attn_w[layer_idx], feed_w[layer_idx]
        w_qkv, w_out = w_attn[:, : 3 * part], w_attn[:, 3 * part :]
        w_expand, w_contract = w_feed[:, :hidden_part], w_feed[:, hidden_part:]
        b_query = bias_of(layer_idx, 0, small).astype(jnp.float32)
        b_value = bias_of(layer_idx, small, small).astype(jnp.float32)
        b_out = bias_of(layer_idx, 2 * small, small)
        b_contract = bias_of(layer_idx, 3 * small, small)
        b_expand = bias_of(layer_idx, 4 * small, hidden_part // row_count)
        gain_two = feed_gain[layer_idx].astype(jnp.float32)[None]
        shift_two = feed_shift[layer_idx].astype(jnp.float32)[None]
        b_qkv = jnp.concatenate([b_query, jnp.zeros_like(b_query), b_value])
        qkv = (jnp.dot(norm_one, w_qkv, preferred_element_type=jnp.float32) + b_qkv).astype(
            jnp.bfloat16
        )
        query_rows, key_rows, value_rows = (
            qkv[:, :part],
            qkv[:, part : 2 * part],
            qkv[:, 2 * part :],
        )
        mixed_rows, log_totals = attend(query_rows, key_rows, value_rows)
        partial_rows = contract_cols(mixed_rows, w_out) + spread_bias(b_out, width)
        resid, norm_two, unit_two, inv_two = exchange(
            "forward", partial_rows.astype(jnp.bfloat16), resid, gain_two, shift_two
        )
        before_act = jnp.dot(norm_two, w_expand, preferred_element_type=jnp.float32) + b_expand
        hidden_rows = gelu_tanh(before_act).astype(jnp.bfloat16)
        partial_rows = contract_cols(hidden_rows, w_contract) + spread_bias(b_contract, width)
        saved.append(
            (
                (w_qkv, w_out, w_expand, w_contract, gain_two),
                (norm_one, unit_one, inv_one, query_rows, key_rows, value_rows),
                (mixed_rows, log_totals, norm_two, unit_two, inv_two, before_act, hidden_rows),
            )
        )
        if layer_idx + 1 < layer_count:
            resid, norm_one, unit_one, inv_one = exchange(
                "forward",
                partial_rows.astype(jnp.bfloat16),
                resid,
                gain_of[layer_idx + 1],
                shift_of[layer_idx + 1],
            )
        else:
            count = resid.shape[0]
            start = lax.axis_index("col") * count
            mine = lax.dynamic_slice_in_dim(partial_rows, start, count, 0) + resid
            partial_rows = lax.dynamic_update_slice_in_dim(partial_rows, mine, start, 0)
            outputs = lax.psum_scatter(
                partial_rows.astype(jnp.bfloat16), "col", scatter_dimension=1, tiled=True
            ).T
    grad = own_rows(cot_full).astype(jnp.float32)
    branch_full = cot_full
    packs = [None] * layer_count
    vectors = [None] * layer_count
    norm_sums = [None] * layer_count
    for layer_idx in reversed(range(layer_count)):
        (
            (w_qkv, w_out, w_expand, w_contract, gain_two),
            (norm_one, unit_one, inv_one, query_rows, key_rows, value_rows),
            (mixed_rows, log_totals, norm_two, unit_two, inv_two, before_act, hidden_rows),
        ) = saved[layer_idx]
        d_hidden = jnp.dot(branch_full, w_contract, preferred_element_type=jnp.float32)
        d_before = jax.vjp(gelu_tanh, before_act)[1](d_hidden)[0].astype(jnp.bfloat16)
        d_partial = contract_cols(d_before, w_expand).astype(jnp.bfloat16)
        contract_part = contract_rows(branch_full, hidden_rows)
        expand_part = contract_rows(norm_two, d_before)
        contract_bias_part = token_sum(own_features(branch_full))
        grad, branch_full, gain_two_part, shift_two_part = exchange(
            "backward", d_partial, grad, gain_two, unit_two, inv_two
        )
        d_mixed = jnp.dot(branch_full, w_out, preferred_element_type=jnp.float32).astype(
            jnp.bfloat16
        )
        out_part = contract_rows(branch_full, mixed_rows)
        out_bias_part = token_sum(own_features(branch_full))
        d_query, d_key, d_value = attend_back(query_rows, key_rows, value_rows, log_totals, d_mixed)
        d_qkv = jnp.concatenate([d_query, d_key, d_value], axis=1)
        d_partial = contract_cols(d_qkv, w_qkv).astype(jnp.bfloat16)
        qkv_part = contract_rows(norm_one, d_qkv)
        grad, branch_full, gain_one_part, shift_one_part = exchange(
            "backward", d_partial, grad, gain_of[layer_idx], unit_one, inv_one
        )
        packs[layer_idx] = jnp.concatenate([qkv_part, out_part, expand_part, contract_part], axis=1)
        vectors[layer_idx] = (
            token_sum(d_query),
            token_sum(d_value),
            out_bias_part,
            token_sum(d_before),
            contract_bias_part,
        )
        norm_sums[layer_idx] = jnp.concatenate(
            [gain_one_part, shift_one_part, gain_two_part, shift_two_part]
        )
    inputs_grad = own_features(branch_full).astype(jnp.float32).T
    norm_total = own_features(lax.psum(jnp.stack(norm_sums), "col"))
    flat = []
    for layer_idx in range(layer_count):
        flat += [by_row(item) for item in vectors[layer_idx]]
        flat += [by_row(norm_total[layer_idx, item]) for item in range(4)]
    sizes = [item.shape[1] for item in flat]
    flat = jnp.concatenate(flat, axis=1)
    pack_width = packs[0].shape[1]
    extra = -(-flat.shape[1] // (pack_width * 16)) * 16
    flat = jnp.pad(flat, ((0, 0), (0, extra * pack_width - flat.shape[1])))
    last_pack = jnp.concatenate(
        [
            packs[0].reshape(row_count, slab, pack_width),
            flat.reshape(row_count, extra, pack_width),
        ],
        axis=1,
    )
    last_total = row_total(last_pack)[0]
    totals = [last_total[:slab]] + [row_total(packs[item]) for item in range(1, layer_count)]
    loose = last_total[slab:].reshape(-1)
    pieces = []
    start = 0
    for size in sizes:
        pieces.append(loose[start : start + size])
        start += size

    def weight_grad(start, count):
        return jnp.stack([item[:, start : start + count] for item in totals])

    def vector_grad(member):
        return jnp.stack([pieces[layer * 9 + member].reshape(1, -1) for layer in range(layer_count)])

    return (
        outputs,
        inputs_grad,
        weight_grad(0, part),
        weight_grad(part, part),
        weight_grad(2 * part, part),
        weight_grad(3 * part, part),
        vector_grad(0),
        vector_grad(1),
        vector_grad(2),
        vector_grad(5),
        vector_grad(6),
        weight_grad(4 * part, hidden_part),
        vector_grad(3),
        weight_grad(4 * part + hidden_part, hidden_part),
        vector_grad(4),
        vector_grad(7),
        vector_grad(8),
    )


def split_heads(rows_in):
    return rows_in.reshape(rows_in.shape[0] // SEQ, SEQ, rows_in.shape[1] // HD, HD)


def causal_scores(query_block, key_block, row_begin):
    scores = (
        jnp.einsum("sqhd,skhd->shqk", query_block, key_block, preferred_element_type=jnp.float32)
        * 0.125
    )
    grid_shape = (query_block.shape[1], key_block.shape[1])
    row_ids = row_begin + lax.broadcasted_iota(jnp.int32, grid_shape, 0)
    col_ids = lax.broadcasted_iota(jnp.int32, grid_shape, 1)
    return jnp.where((row_ids >= col_ids)[None, None], scores, NEG_FILL)


def attend(query_rows, key_rows, value_rows):
    block_rows = min(512, SEQ)
    query_seq = split_heads(query_rows)
    key_seq = split_heads(key_rows)
    value_seq = split_heads(value_rows)
    out_blocks = []
    log_totals = []
    for row_begin in range(0, SEQ, block_rows):
        row_end = row_begin + block_rows
        scores = causal_scores(query_seq[:, row_begin:row_end], key_seq[:, :row_end], row_begin)
        row_top = jnp.max(scores, axis=-1, keepdims=True)
        weights = jnp.exp(scores - row_top)
        row_total = jnp.sum(weights, axis=-1, keepdims=True)
        prob_rows = (weights / row_total).astype(jnp.bfloat16)
        out_blocks.append(
            jnp.einsum(
                "shqk,skhd->sqhd",
                prob_rows,
                value_seq[:, :row_end],
                preferred_element_type=jnp.float32,
            )
        )
        log_totals.append(row_top + jnp.log(row_total))
    mixed_rows = jnp.concatenate(out_blocks, axis=1).reshape(query_rows.shape).astype(jnp.bfloat16)
    return (mixed_rows, log_totals)


def attend_back(query_rows, key_rows, value_rows, log_totals, d_mixed):
    block_rows = min(512, SEQ)
    query_seq = split_heads(query_rows)
    key_seq = split_heads(key_rows)
    value_seq = split_heads(value_rows)
    grad_seq = split_heads(d_mixed)
    d_query_blocks = []
    d_key_seq = jnp.zeros(key_seq.shape, jnp.float32)
    d_value_seq = jnp.zeros(value_seq.shape, jnp.float32)
    for block_idx, row_begin in enumerate(range(0, SEQ, block_rows)):
        row_end = row_begin + block_rows
        tail_pad = ((0, 0), (0, SEQ - row_end), (0, 0), (0, 0))
        scores = causal_scores(query_seq[:, row_begin:row_end], key_seq[:, :row_end], row_begin)
        prob_rows = jnp.exp(scores - log_totals[block_idx])
        grad_block = grad_seq[:, row_begin:row_end]
        d_probs = jnp.einsum(
            "sqhd,skhd->shqk",
            grad_block,
            value_seq[:, :row_end],
            preferred_element_type=jnp.float32,
        )
        d_value_seq = d_value_seq + jnp.pad(
            jnp.einsum(
                "shqk,sqhd->skhd",
                prob_rows.astype(jnp.bfloat16),
                grad_block,
                preferred_element_type=jnp.float32,
            ),
            tail_pad,
        )
        inner_sum = jnp.sum(d_probs * prob_rows, axis=-1, keepdims=True)
        d_scores = (prob_rows * (d_probs - inner_sum)).astype(jnp.bfloat16)
        d_query_blocks.append(
            jnp.einsum(
                "shqk,skhd->sqhd",
                d_scores,
                key_seq[:, :row_end],
                preferred_element_type=jnp.float32,
            )
            * 0.125
        )
        d_key_seq = d_key_seq + jnp.pad(
            jnp.einsum(
                "shqk,sqhd->skhd",
                d_scores,
                query_seq[:, row_begin:row_end],
                preferred_element_type=jnp.float32,
            )
            * 0.125,
            tail_pad,
        )
    rows_shape = query_rows.shape
    d_query = jnp.concatenate(d_query_blocks, axis=1).reshape(rows_shape).astype(jnp.bfloat16)
    return (
        d_query,
        d_key_seq.reshape(rows_shape).astype(jnp.bfloat16),
        d_value_seq.reshape(rows_shape).astype(jnp.bfloat16),
    )


def solution(mesh):
    placed = (
        P("col", "row"),
        P("col", "row"),
        P(None, "row", "col"),
        P(None, "row", "col"),
        P(None, "row", "col"),
        P(None, "row", "col"),
        P(None, "col", "row"),
        P(None, "col", "row"),
        P(None, "col", "row"),
        P(),
        P(),
        P(None, "row", "col"),
        P(None, "col", "row"),
        P(None, "row", "col"),
        P(None, "col", "row"),
        P(),
        P(),
    )
    return jax.shard_map(
        local,
        mesh=mesh,
        in_specs=placed,
        out_specs=(
            P("col", "row"),
            P("col", "row"),
            P(None, "row", "col"),
            P(None, "row", "col"),
            P(None, "row", "col"),
            P(None, "row", "col"),
            P(None, "col", "row"),
            P(None, "col", "row"),
            P(None, "col", "row"),
            P(None, "col", "row"),
            P(None, "col", "row"),
            P(None, "row", "col"),
            P(None, "col", "row"),
            P(None, "row", "col"),
            P(None, "col", "row"),
            P(None, "col", "row"),
            P(None, "col", "row"),
        ),
        check_vma=False,
    )
```

```python
import functools

import jax
import jax.numpy as jnp
from jax import lax
from jax.experimental import pallas as pl
from jax.experimental.pallas import tpu as pltpu
from jax.sharding import PartitionSpec as P

HD = 64
SEQ = 1024


EPSILON = 1e-05
NEG_FILL = -1e30


def contract_rows(left, right):
    return lax.dot_general(
        left, right, (((0,), (0,)), ((), ())), preferred_element_type=jnp.float32
    )


def contract_cols(left, right):
    return lax.dot_general(
        left, right, (((1,), (1,)), ((), ())), preferred_element_type=jnp.float32
    )


def gelu_tanh(values):
    return (
        0.5
        * values
        * (1.0 + jnp.tanh(0.7978845608028654 * (values + 0.044715 * values * values * values)))
    )


def col_gather(rows_in):
    return lax.all_gather(rows_in, "col", axis=0, tiled=True)


def col_scatter(partial_rows):
    return lax.psum_scatter(
        partial_rows.astype(jnp.bfloat16), "col", scatter_dimension=0, tiled=True
    ).astype(jnp.float32)


def own_rows(rows_in):
    count = rows_in.shape[0] // lax.axis_size("col")
    return lax.dynamic_slice_in_dim(rows_in, lax.axis_index("col") * count, count, 0)


def own_features(rows_in):
    width = rows_in.shape[-1] // lax.axis_size("col")
    return lax.dynamic_slice_in_dim(
        rows_in, lax.axis_index("col") * width, width, rows_in.ndim - 1
    )


def spread_bias(bias_share, full_width):
    return lax.dynamic_update_slice_in_dim(
        jnp.zeros((full_width,), jnp.float32),
        bias_share.astype(jnp.float32),
        lax.axis_index("col") * bias_share.shape[0],
        0,
    )


def norm_unit(rows_in):
    row_mean = jnp.mean(rows_in, axis=1, keepdims=True)
    centred = rows_in - row_mean
    inv_std = lax.rsqrt(jnp.mean(centred * centred, axis=1, keepdims=True) + EPSILON)
    return centred * inv_std, inv_std


def norm_apply(unit_rows, gain, shift):
    return (unit_rows * gain + shift).astype(jnp.bfloat16)


def norm_back(normed_grad, unit_rows, inv_std, gain):
    scaled = normed_grad * gain
    first = jnp.mean(scaled, axis=1, keepdims=True)
    second = jnp.mean(scaled * unit_rows, axis=1, keepdims=True)
    back_rows = inv_std * (scaled - first - unit_rows * second)
    return back_rows, jnp.sum(normed_grad * unit_rows, axis=0), jnp.sum(normed_grad, axis=0)


def token_sum(rows_in):
    return jnp.sum(rows_in.astype(jnp.float32), axis=0)


def exchange_body(kind, chunks, *refs):
    if kind == "forward":
        partial, carry, gain, shift, carry_out, full, unit_out, inv_out = refs[:8]
        scratch = refs[8:]
    else:
        partial, carry, gain, unit, inv, carry_out, full, sums_out = refs[:8]
        scratch, (sums, sums_s, sums_r) = refs[8:-3], refs[-3:]
    from_pair, pair_sum, from_far = scratch[:3]
    (near_s, near_r, far_s, far_r, gy_s, gy_r, gc_s, gc_r, fw_s, fw_r) = scratch[3:]
    rows = carry.shape[0]
    step = rows // chunks
    me = lax.axis_index("col")
    pair = me + 1 - 2 * (me % 2)
    far = (me + 2) % 4
    corner = (pair + 2) % 4

    def at(block, chunk):
        return pl.ds(pl.multiple_of(block * rows + chunk * step, step), step)

    def send(src, dst, send_sem, recv_sem, target):
        return pltpu.make_async_remote_copy(
            src_ref=src,
            dst_ref=dst,
            send_sem=send_sem,
            recv_sem=recv_sem,
            device_id={"col": target},
            device_id_type=pl.DeviceIdType.MESH,
        )

    barrier = pltpu.get_barrier_semaphore()
    greeted = (pair, far) if kind == "forward" else (pair, far, corner)
    for other in greeted:
        pl.semaphore_signal(
            barrier, inc=1, device_id={"col": other}, device_id_type=pl.DeviceIdType.MESH
        )
    pl.semaphore_wait(barrier, len(greeted))
    near = []
    for half, owner in enumerate((corner, pair)):
        for chunk in range(chunks):
            slot = half * chunks + chunk
            copy = send(
                partial.at[at(owner, chunk)],
                from_pair.at[pl.ds(slot * step, step)],
                near_s.at[slot],
                near_r.at[slot],
                pair,
            )
            copy.start()
            near.append(copy)
    over = []
    for chunk in range(chunks):
        near[chunk].wait_recv()
        here = pl.ds(chunk * step, step)
        pair_sum[here] = (
            partial[at(far, chunk)].astype(jnp.float32) + from_pair[here].astype(jnp.float32)
        ).astype(jnp.bfloat16)
        copy = send(pair_sum.at[here], from_far.at[here], far_s.at[chunk], far_r.at[chunk], far)
        copy.start()
        over.append(copy)
    if kind == "backward":
        gain_sum = jnp.zeros((1, carry.shape[1]), jnp.float32)
        shift_sum = jnp.zeros((1, carry.shape[1]), jnp.float32)
    across = []
    beside = []
    for chunk in range(chunks):
        near[chunks + chunk].wait_recv()
        over[chunk].wait_recv()
        here = pl.ds(chunk * step, step)
        total = (
            partial[at(me, chunk)].astype(jnp.float32)
            + from_pair[pl.ds((chunks + chunk) * step, step)].astype(jnp.float32)
            + from_far[here].astype(jnp.float32)
        )
        if kind == "forward":
            value = carry[here] + total
            carry_out[here] = value
            unit_rows, inv_std = norm_unit(value)
            unit_out[here] = unit_rows
            inv_out[here] = jnp.broadcast_to(inv_std, (step, inv_out.shape[1]))
            result = norm_apply(unit_rows, gain[...], shift[...])
        else:
            unit_rows = unit[here]
            gain_sum = gain_sum + jnp.sum(total * unit_rows, axis=0, keepdims=True)
            shift_sum = shift_sum + jnp.sum(total, axis=0, keepdims=True)
            scaled = total * gain[...]
            first = jnp.mean(scaled, axis=1, keepdims=True)
            second = jnp.mean(scaled * unit_rows, axis=1, keepdims=True)
            value = carry[here] + inv[here][:, :1] * (scaled - first - unit_rows * second)
            carry_out[here] = value
            result = value.astype(jnp.bfloat16)
        mine = at(me, chunk)
        full[mine] = result
        copy = send(full.at[mine], full.at[mine], gy_s.at[chunk], gy_r.at[chunk], far)
        copy.start()
        across.append(copy)
        copy = send(full.at[mine], full.at[mine], gc_s.at[chunk], gc_r.at[chunk], pair)
        copy.start()
        beside.append(copy)
    if kind == "backward":
        sums[me] = jnp.concatenate(
            [gain_sum, shift_sum, jnp.zeros((6, gain_sum.shape[1]), jnp.float32)], axis=0
        )
        small = []
        for slot, other in enumerate(greeted):
            copy = send(sums.at[me], sums.at[me], sums_s.at[slot], sums_r.at[slot], other)
            copy.start()
            small.append(copy)
    onward = []
    for chunk in range(chunks):
        across[chunk].wait_recv()
        spot = at(far, chunk)
        copy = send(full.at[spot], full.at[spot], fw_s.at[chunk], fw_r.at[chunk], pair)
        copy.start()
        onward.append(copy)
    for copy in beside + onward:
        copy.wait_recv()
    if kind == "backward":
        for copy in small:
            copy.wait_recv()
        sums_out[...] = sums[0] + sums[1] + sums[2] + sums[3]
        onward = onward + small
    for copy in near + over + across + beside + onward:
        copy.wait_send()


def exchange(kind, partial, carry, *rest):
    rows, width = carry.shape
    chunks = 4
    wide = jax.ShapeDtypeStruct((rows, width), jnp.float32)
    outs = [wide, jax.ShapeDtypeStruct((4 * rows, width), jnp.bfloat16)]
    if kind == "forward":
        outs += [wide, jax.ShapeDtypeStruct((rows, 128), jnp.float32)]
    else:
        outs += [jax.ShapeDtypeStruct((8, width), jnp.float32)]
    in_vmem = pl.BlockSpec(memory_space=pltpu.VMEM)
    dma = pltpu.SemaphoreType.DMA
    return pl.pallas_call(
        functools.partial(exchange_body, kind, chunks),
        out_shape=outs,
        in_specs=[in_vmem] * (2 + len(rest)),
        out_specs=[in_vmem] * len(outs),
        scratch_shapes=[
            pltpu.VMEM((2 * rows, width), jnp.bfloat16),
            pltpu.VMEM((rows, width), jnp.bfloat16),
            pltpu.VMEM((rows, width), jnp.bfloat16),
        ]
        + [dma((2 * chunks,))] * 2
        + [dma((chunks,))] * 8
        + (
            []
            if kind == "forward"
            else [pltpu.VMEM((4, 8, width), jnp.float32), dma((3,)), dma((3,))]
        ),
        cost_estimate=pl.CostEstimate(
            flops=20 * rows * width, bytes_accessed=50_000_000, transcendentals=0
        ),
        compiler_params=pltpu.CompilerParams(
            collective_id=1 if kind == "forward" else 2,
            has_side_effects=True,
            vmem_limit_bytes=32 * 1024 * 1024,
        ),
        name="exchange_" + kind,
    )(partial, carry, *rest)


def gather_body(chunks, block, full, gy_s, gy_r, gc_s, gc_r, fw_s, fw_r):
    rows = block.shape[0]
    step = rows // chunks
    me = lax.axis_index("col")
    pair = me + 1 - 2 * (me % 2)
    far = (me + 2) % 4

    def at(owner, chunk):
        return pl.ds(pl.multiple_of(owner * rows + chunk * step, step), step)

    def send(src, dst, send_sem, recv_sem, target):
        return pltpu.make_async_remote_copy(
            src_ref=src,
            dst_ref=dst,
            send_sem=send_sem,
            recv_sem=recv_sem,
            device_id={"col": target},
            device_id_type=pl.DeviceIdType.MESH,
        )

    barrier = pltpu.get_barrier_semaphore()
    for other in (pair, far):
        pl.semaphore_signal(
            barrier, inc=1, device_id={"col": other}, device_id_type=pl.DeviceIdType.MESH
        )
    pl.semaphore_wait(barrier, 2)
    across, beside, onward = [], [], []
    for chunk in range(chunks):
        here = block.at[pl.ds(chunk * step, step)]
        mine = full.at[at(me, chunk)]
        across.append(send(here, mine, gy_s.at[chunk], gy_r.at[chunk], far))
        across[-1].start()
        beside.append(send(here, mine, gc_s.at[chunk], gc_r.at[chunk], pair))
        beside[-1].start()
    full[pl.ds(pl.multiple_of(me * rows, rows), rows)] = block[...]
    for chunk in range(chunks):
        across[chunk].wait_recv()
        spot = full.at[at(far, chunk)]
        onward.append(send(spot, spot, fw_s.at[chunk], fw_r.at[chunk], pair))
        onward[-1].start()
    for copy in beside + onward:
        copy.wait_recv()
    for copy in across + beside + onward:
        copy.wait_send()


def first_gather(block):
    chunks = 4
    rows, width = block.shape
    in_vmem = pl.BlockSpec(memory_space=pltpu.VMEM)
    return pl.pallas_call(
        functools.partial(gather_body, chunks),
        out_shape=jax.ShapeDtypeStruct((4 * rows, width), block.dtype),
        in_specs=[in_vmem],
        out_specs=in_vmem,
        scratch_shapes=[pltpu.SemaphoreType.DMA((chunks,))] * 6,
        cost_estimate=pl.CostEstimate(flops=0, bytes_accessed=30_000_000, transcendentals=0),
        compiler_params=pltpu.CompilerParams(
            collective_id=3, has_side_effects=True, vmem_limit_bytes=32 * 1024 * 1024
        ),
        name="first_gather",
    )(block)


def row_sum_body(count, weights, loose, weights_out, loose_out, packed, landed, send_sem, recv_sem):
    slab = weights.shape[1]
    head = loose.shape[1]
    me = lax.axis_index("row")

    def copy_to(offset):
        target = (me + offset) % count
        return pltpu.make_async_remote_copy(
            src_ref=packed.at[offset],
            dst_ref=landed.at[offset],
            send_sem=send_sem.at[offset],
            recv_sem=recv_sem.at[offset],
            device_id={"row": target},
            device_id_type=pl.DeviceIdType.MESH,
        )

    barrier = pltpu.get_barrier_semaphore()

    def greet(offset, carry):
        pl.semaphore_signal(
            barrier,
            inc=1,
            device_id={"row": (me + offset) % count},
            device_id_type=pl.DeviceIdType.MESH,
        )
        return carry

    lax.fori_loop(1, count, greet, 0)
    pl.semaphore_wait(barrier, count - 1)

    def launch(offset, carry):
        target = (me + offset) % count
        packed[offset, :head] = loose[target].astype(jnp.bfloat16)
        packed[offset, head : head + slab] = weights[target].astype(jnp.bfloat16)
        if packed.shape[1] > head + slab:
            packed[offset, head + slab :] = jnp.zeros(
                (packed.shape[1] - head - slab, packed.shape[2]), jnp.bfloat16
            )
        copy_to(offset).start()
        return carry

    lax.fori_loop(1, count, launch, 0)
    weights_out[...] = weights[me]
    loose_out[...] = loose[me]

    def collect(offset, carry):
        copy_to(offset).wait_recv()
        loose_out[...] += landed[offset, :head].astype(jnp.float32)
        weights_out[...] += landed[offset, head : head + slab].astype(jnp.float32)
        copy_to(offset).wait_send()
        return carry

    lax.fori_loop(1, count, collect, 0)


def row_sum(weights, loose):
    count, slab, width = weights.shape
    head = loose.shape[1]
    block = -(-(head + slab) // 16) * 16
    in_vmem = pl.BlockSpec(memory_space=pltpu.VMEM)
    return pl.pallas_call(
        functools.partial(row_sum_body, count),
        out_shape=[
            jax.ShapeDtypeStruct((slab, width), jnp.float32),
            jax.ShapeDtypeStruct((head, width), jnp.float32),
        ],
        in_specs=[in_vmem] * 2,
        out_specs=[in_vmem] * 2,
        scratch_shapes=[
            pltpu.VMEM((count, block, width), jnp.bfloat16),
            pltpu.VMEM((count, block, width), jnp.bfloat16),
            pltpu.SemaphoreType.DMA((count,)),
            pltpu.SemaphoreType.DMA((count,)),
        ],
        cost_estimate=pl.CostEstimate(flops=0, bytes_accessed=80_000_000, transcendentals=0),
        compiler_params=pltpu.CompilerParams(
            collective_id=4, has_side_effects=True, vmem_limit_bytes=40 * 1024 * 1024
        ),
        name="row_sum",
    )(weights, loose)


def by_row(vector):
    return vector.reshape(lax.axis_size("row"), -1)


def row_total(packed):
    return lax.psum_scatter(
        packed.astype(jnp.bfloat16), "row", scatter_dimension=0, tiled=True
    ).astype(jnp.float32)


def local(
    inputs,
    cotangent,
    query_weight,
    key_weight,
    value_weight,
    out_weight,
    query_bias,
    value_bias,
    out_bias,
    attention_gain,
    attention_shift,
    expand_weight,
    expand_bias,
    contract_weight,
    contract_bias,
    feed_gain,
    feed_shift,
):
    layer_count, slab, part = query_weight.shape
    hidden_part = expand_weight.shape[2]
    row_count = lax.axis_size("row")
    width = slab * row_count
    bias_pack = jnp.concatenate(
        [
            item.reshape(layer_count, -1)
            for item in (query_bias, value_bias, out_bias, contract_bias, expand_bias)
        ],
        axis=1,
    )
    bias_len = bias_pack.size
    attn_width = 4 * part
    bias_rows = -(-bias_len // (attn_width * 16)) * 16
    bias_block = jnp.pad(
        bias_pack.reshape(-1), (0, bias_rows * attn_width - bias_len)
    ).reshape(bias_rows, attn_width)

    def attn_slab(layer_idx):
        return jnp.concatenate(
            [
                query_weight[layer_idx],
                key_weight[layer_idx],
                value_weight[layer_idx],
                out_weight[layer_idx],
            ],
            axis=1,
        )

    first_pack = lax.all_gather(
        jnp.concatenate([attn_slab(0), bias_block], axis=0), "row", axis=0
    )
    gathered_bias = (
        first_pack[:, slab:].reshape(row_count, -1)[:, :bias_len].reshape(row_count, layer_count, -1)
    )
    small = part // row_count
    feed_slabs = [
        jnp.concatenate([expand_weight[item], contract_weight[item]], axis=1)
        for item in range(layer_count)
    ]
    attn_w = [first_pack[:, :slab].reshape(width, attn_width)]
    feed_w = [lax.all_gather(feed_slabs[0], "row", axis=0, tiled=True)]
    for layer_idx in range(1, layer_count):
        attn_w.append(lax.all_gather(attn_slab(layer_idx), "row", axis=0, tiled=True))
        feed_w.append(lax.all_gather(feed_slabs[layer_idx], "row", axis=0, tiled=True))

    def bias_of(layer_idx, start, count):
        return gathered_bias[:, layer_idx, start : start + count].reshape(-1)

    x_full = first_gather(inputs).T
    resid = own_rows(x_full).astype(jnp.float32)
    unit_one, inv_one = norm_unit(resid)
    inv_one = jnp.broadcast_to(inv_one, (resid.shape[0], 128))
    gain_of = [item.astype(jnp.float32)[None] for item in attention_gain]
    shift_of = [item.astype(jnp.float32)[None] for item in attention_shift]
    norm_one = norm_apply(norm_unit(x_full.astype(jnp.float32))[0], gain_of[0], shift_of[0])
    saved = []
    for layer_idx in range(layer_count):
        w_attn, w_feed = attn_w[layer_idx], feed_w[layer_idx]
        w_qkv, w_out = w_attn[:, : 3 * part], w_attn[:, 3 * part :]
        w_expand, w_contract = w_feed[:, :hidden_part], w_feed[:, hidden_part:]
        b_query = bias_of(layer_idx, 0, small).astype(jnp.float32)
        b_value = bias_of(layer_idx, small, small).astype(jnp.float32)
        b_out = bias_of(layer_idx, 2 * small, small)
        b_contract = bias_of(layer_idx, 3 * small, small)
        b_expand = bias_of(layer_idx, 4 * small, hidden_part // row_count)
        gain_two = feed_gain[layer_idx].astype(jnp.float32)[None]
        shift_two = feed_shift[layer_idx].astype(jnp.float32)[None]
        b_qkv = jnp.concatenate([b_query, jnp.zeros_like(b_query), b_value])
        qkv = (jnp.dot(norm_one, w_qkv, preferred_element_type=jnp.float32) + b_qkv).astype(
            jnp.bfloat16
        )
        query_rows, key_rows, value_rows = (
            qkv[:, :part],
            qkv[:, part : 2 * part],
            qkv[:, 2 * part :],
        )
        mixed_rows, log_totals = attend(query_rows, key_rows, value_rows)
        partial_rows = contract_cols(mixed_rows, w_out) + spread_bias(b_out, width)
        resid, norm_two, unit_two, inv_two = exchange(
            "forward", partial_rows.astype(jnp.bfloat16), resid, gain_two, shift_two
        )
        if layer_idx == 0:
            held, norm_two = lax.optimization_barrier((cotangent, norm_two))
            cot_full = lax.all_gather(held, "col", axis=0, tiled=True).T
        before_act = jnp.dot(norm_two, w_expand, preferred_element_type=jnp.float32) + b_expand
        hidden_rows = gelu_tanh(before_act).astype(jnp.bfloat16)
        partial_rows = contract_cols(hidden_rows, w_contract) + spread_bias(b_contract, width)
        saved.append(
            (
                (w_qkv, w_out, w_expand, w_contract, gain_two),
                (norm_one, unit_one, inv_one, query_rows, key_rows, value_rows),
                (mixed_rows, log_totals, norm_two, unit_two, inv_two, before_act, hidden_rows),
            )
        )
        if layer_idx + 1 < layer_count:
            resid, norm_one, unit_one, inv_one = exchange(
                "forward",
                partial_rows.astype(jnp.bfloat16),
                resid,
                gain_of[layer_idx + 1],
                shift_of[layer_idx + 1],
            )
        else:
            count = resid.shape[0]
            start = lax.axis_index("col") * count
            mine = lax.dynamic_slice_in_dim(partial_rows, start, count, 0) + resid
            partial_rows = lax.dynamic_update_slice_in_dim(partial_rows, mine, start, 0)
            outputs = lax.psum_scatter(
                partial_rows.astype(jnp.bfloat16), "col", scatter_dimension=1, tiled=True
            ).T
    grad = own_rows(cot_full).astype(jnp.float32)
    branch_full = cot_full
    packs = [None] * layer_count
    vectors = [None] * layer_count
    norm_sums = [None] * layer_count
    for layer_idx in reversed(range(layer_count)):
        (
            (w_qkv, w_out, w_expand, w_contract, gain_two),
            (norm_one, unit_one, inv_one, query_rows, key_rows, value_rows),
            (mixed_rows, log_totals, norm_two, unit_two, inv_two, before_act, hidden_rows),
        ) = saved[layer_idx]
        d_hidden = jnp.dot(branch_full, w_contract, preferred_element_type=jnp.float32)
        d_before = jax.vjp(gelu_tanh, before_act)[1](d_hidden)[0].astype(jnp.bfloat16)
        d_partial = contract_cols(d_before, w_expand).astype(jnp.bfloat16)
        contract_part = contract_rows(branch_full, hidden_rows)
        expand_part = contract_rows(norm_two, d_before)
        contract_bias_part = token_sum(own_features(branch_full))
        grad, branch_full, two_sums = exchange(
            "backward", d_partial, grad, gain_two, unit_two, inv_two
        )
        d_mixed = jnp.dot(branch_full, w_out, preferred_element_type=jnp.float32).astype(
            jnp.bfloat16
        )
        out_part = contract_rows(branch_full, mixed_rows)
        out_bias_part = token_sum(own_features(branch_full))
        d_query, d_key, d_value = attend_back(query_rows, key_rows, value_rows, log_totals, d_mixed)
        d_qkv = jnp.concatenate([d_query, d_key, d_value], axis=1)
        d_partial = contract_cols(d_qkv, w_qkv).astype(jnp.bfloat16)
        if layer_idx + 1 == layer_count:
            outputs, d_partial = lax.optimization_barrier((outputs, d_partial))
        qkv_part = contract_rows(norm_one, d_qkv)
        grad, branch_full, one_sums = exchange(
            "backward", d_partial, grad, gain_of[layer_idx], unit_one, inv_one
        )
        packs[layer_idx] = (qkv_part, out_part, expand_part, contract_part)
        vectors[layer_idx] = (
            token_sum(d_query),
            token_sum(d_value),
            out_bias_part,
            token_sum(d_before),
            contract_bias_part,
        )
        norm_sums[layer_idx] = jnp.concatenate(
            [one_sums[:2], two_sums[:2]]
        )
    inputs_grad = own_features(branch_full).astype(jnp.float32).T
    norm_total = own_features(jnp.stack(norm_sums))
    flat = []
    for layer_idx in range(layer_count):
        flat += [by_row(item) for item in vectors[layer_idx]]
        flat += [by_row(norm_total[layer_idx, item]) for item in range(4)]
    sizes = [item.shape[1] for item in flat]
    flat = jnp.concatenate(flat, axis=1)
    qkv_width = 3 * part
    head = -(-flat.shape[1] // (qkv_width * 16)) * 16
    flat = jnp.pad(flat, ((0, 0), (0, head * qkv_width - flat.shape[1])))
    qkv_total, loose = row_sum(
        packs[0][0].reshape(row_count, slab, qkv_width), flat.reshape(row_count, head, qkv_width)
    )
    loose = loose.reshape(-1)
    last = layer_count - 1
    feed_total = row_total(jnp.concatenate(packs[last][2:], axis=1))
    others = []
    for layer_idx in range(layer_count):
        others.append(packs[layer_idx][1])
        if layer_idx > 0:
            others.append(packs[layer_idx][0])
        if layer_idx < last:
            others += packs[layer_idx][2:]
    joined = row_total(jnp.concatenate(others, axis=1))
    totals = []
    start = 0
    for layer_idx in range(layer_count):
        out_total = joined[:, start : start + part]
        start += part
        if layer_idx > 0:
            qkv_total = joined[:, start : start + qkv_width]
            start += qkv_width
        if layer_idx < last:
            feed_now = joined[:, start : start + 2 * hidden_part]
            start += 2 * hidden_part
        else:
            feed_now = feed_total
        totals.append(jnp.concatenate([qkv_total, out_total, feed_now], axis=1))
    pieces = []
    start = 0
    for size in sizes:
        pieces.append(loose[start : start + size])
        start += size

    def weight_grad(start, count):
        return jnp.stack([item[:, start : start + count] for item in totals])

    def vector_grad(member):
        return jnp.stack([pieces[layer * 9 + member].reshape(1, -1) for layer in range(layer_count)])

    return (
        outputs,
        inputs_grad,
        weight_grad(0, part),
        weight_grad(part, part),
        weight_grad(2 * part, part),
        weight_grad(3 * part, part),
        vector_grad(0),
        vector_grad(1),
        vector_grad(2),
        vector_grad(5),
        vector_grad(6),
        weight_grad(4 * part, hidden_part),
        vector_grad(3),
        weight_grad(4 * part + hidden_part, hidden_part),
        vector_grad(4),
        vector_grad(7),
        vector_grad(8),
    )


def split_heads(rows_in):
    return rows_in.reshape(rows_in.shape[0] // SEQ, SEQ, rows_in.shape[1] // HD, HD)


def causal_scores(query_block, key_block, row_begin):
    scores = (
        jnp.einsum("sqhd,skhd->shqk", query_block, key_block, preferred_element_type=jnp.float32)
        * 0.125
    )
    grid_shape = (query_block.shape[1], key_block.shape[1])
    row_ids = row_begin + lax.broadcasted_iota(jnp.int32, grid_shape, 0)
    col_ids = lax.broadcasted_iota(jnp.int32, grid_shape, 1)
    return jnp.where((row_ids >= col_ids)[None, None], scores, NEG_FILL)


def attend(query_rows, key_rows, value_rows):
    block_rows = min(512, SEQ)
    query_seq = split_heads(query_rows)
    key_seq = split_heads(key_rows)
    value_seq = split_heads(value_rows)
    out_blocks = []
    log_totals = []
    for row_begin in range(0, SEQ, block_rows):
        row_end = row_begin + block_rows
        scores = causal_scores(query_seq[:, row_begin:row_end], key_seq[:, :row_end], row_begin)
        row_top = jnp.max(scores, axis=-1, keepdims=True)
        weights = jnp.exp(scores - row_top)
        row_total = jnp.sum(weights, axis=-1, keepdims=True)
        prob_rows = (weights / row_total).astype(jnp.bfloat16)
        out_blocks.append(
            jnp.einsum(
                "shqk,skhd->sqhd",
                prob_rows,
                value_seq[:, :row_end],
                preferred_element_type=jnp.float32,
            )
        )
        log_totals.append(row_top + jnp.log(row_total))
    mixed_rows = jnp.concatenate(out_blocks, axis=1).reshape(query_rows.shape).astype(jnp.bfloat16)
    return (mixed_rows, log_totals)


def attend_back(query_rows, key_rows, value_rows, log_totals, d_mixed):
    block_rows = min(512, SEQ)
    query_seq = split_heads(query_rows)
    key_seq = split_heads(key_rows)
    value_seq = split_heads(value_rows)
    grad_seq = split_heads(d_mixed)
    d_query_blocks = []
    d_key_seq = jnp.zeros(key_seq.shape, jnp.float32)
    d_value_seq = jnp.zeros(value_seq.shape, jnp.float32)
    for block_idx, row_begin in enumerate(range(0, SEQ, block_rows)):
        row_end = row_begin + block_rows
        tail_pad = ((0, 0), (0, SEQ - row_end), (0, 0), (0, 0))
        scores = causal_scores(query_seq[:, row_begin:row_end], key_seq[:, :row_end], row_begin)
        prob_rows = jnp.exp(scores - log_totals[block_idx])
        grad_block = grad_seq[:, row_begin:row_end]
        d_probs = jnp.einsum(
            "sqhd,skhd->shqk",
            grad_block,
            value_seq[:, :row_end],
            preferred_element_type=jnp.float32,
        )
        d_value_seq = d_value_seq + jnp.pad(
            jnp.einsum(
                "shqk,sqhd->skhd",
                prob_rows.astype(jnp.bfloat16),
                grad_block,
                preferred_element_type=jnp.float32,
            ),
            tail_pad,
        )
        inner_sum = jnp.sum(d_probs * prob_rows, axis=-1, keepdims=True)
        d_scores = (prob_rows * (d_probs - inner_sum)).astype(jnp.bfloat16)
        d_query_blocks.append(
            jnp.einsum(
                "shqk,skhd->sqhd",
                d_scores,
                key_seq[:, :row_end],
                preferred_element_type=jnp.float32,
            )
            * 0.125
        )
        d_key_seq = d_key_seq + jnp.pad(
            jnp.einsum(
                "shqk,sqhd->skhd",
                d_scores,
                query_seq[:, row_begin:row_end],
                preferred_element_type=jnp.float32,
            )
            * 0.125,
            tail_pad,
        )
    rows_shape = query_rows.shape
    d_query = jnp.concatenate(d_query_blocks, axis=1).reshape(rows_shape).astype(jnp.bfloat16)
    return (
        d_query,
        d_key_seq.reshape(rows_shape).astype(jnp.bfloat16),
        d_value_seq.reshape(rows_shape).astype(jnp.bfloat16),
    )


def solution(mesh):
    placed = (
        P("col", "row"),
        P("col", "row"),
        P(None, "row", "col"),
        P(None, "row", "col"),
        P(None, "row", "col"),
        P(None, "row", "col"),
        P(None, "col", "row"),
        P(None, "col", "row"),
        P(None, "col", "row"),
        P(),
        P(),
        P(None, "row", "col"),
        P(None, "col", "row"),
        P(None, "row", "col"),
        P(None, "col", "row"),
        P(),
        P(),
    )
    return jax.shard_map(
        local,
        mesh=mesh,
        in_specs=placed,
        out_specs=(
            P("col", "row"),
            P("col", "row"),
            P(None, "row", "col"),
            P(None, "row", "col"),
            P(None, "row", "col"),
            P(None, "row", "col"),
            P(None, "col", "row"),
            P(None, "col", "row"),
            P(None, "col", "row"),
            P(None, "col", "row"),
            P(None, "col", "row"),
            P(None, "row", "col"),
            P(None, "col", "row"),
            P(None, "row", "col"),
            P(None, "col", "row"),
            P(None, "col", "row"),
            P(None, "col", "row"),
        ),
        check_vma=False,
    )
```
